32 devices in a mesh: gx: 8 (over z, y), gy: 4 (over x, core).
Axes of the slice: x: 2, y: 2, z: 4, core: 2. Of those that a mesh axis runs over, the one named last changes fastest.
Arguments:
- right_side: float32 [16, 512, 1024], P(None, 'gx', 'gy'), may hold values from -50 to 50
- center: float32 [512, 1024], P('gx', 'gy'), may hold values from 4 to 6
- couplings: float32 [4, 512, 1024], P(None, 'gx', 'gy'), may hold values from 0.1 to 1
Outputs:
- q_basis: float32 [80, 512, 1024], P(None, 'gx', 'gy')
- r_factor: float32 [80, 80], replicated
The draws below stay inside these ranges and needn't reach their ends.
All inputs are finite; a program needn't handle non-finite values.
Results may differ from the reference program's by a relative error of at most 0.0003.
Values sent between devices are 32-bit elements; how exact they have to be, the bound alone decides.
A program may use at most 64 MiB of HBM per device.

```python
import math
import jax
import jax.numpy as jnp
from jax import lax

B = 16
S = 4
COLS = 80
NX = 512
NY = 1024


def draw_right_side(key, part):
    key_common, key_own, key_cell, key_scen = jax.random.split(key, 4)
    common = jax.random.truncated_normal(key_common, -4.0, 4.0, (NX, NY), jnp.float32)
    own = jax.random.truncated_normal(key_own, -4.0, 4.0, (B, NX, NY), jnp.float32)
    mixing = 0.05
    growth = 2.0
    base_values = common[None] + mixing * own
    cell_scale = 0.25 * jnp.exp(jax.random.uniform(key_cell, (NX, NY), jnp.float32) * math.log(10.0))
    scen_scale = 0.3 * jnp.exp(jax.random.uniform(key_scen, (B, 1, 1), jnp.float32) * math.log(10.0))
    position = jnp.arange(NX, dtype=jnp.float32) / NX
    envelope = (1.0 + growth * position) / (1.0 + growth / 2.0)
    return base_values * cell_scale[None] * scen_scale * envelope[None, :, None]


def level_of(key, shape, cuts, smallest, high):
    def one(dim, parts):
        heights = jax.random.uniform(jax.random.fold_in(jax.random.fold_in(key, 6), dim), (parts,), jnp.float32, smallest / len(cuts), high / len(cuts))
        return jnp.repeat(jnp.exp(heights), shape[dim] // parts).reshape((-1,) + (1,) * (len(shape) - dim - 1))

    factor_of = one(*cuts[0])
    for cut in cuts[1:]:
        factor_of = factor_of * one(*cut)
    return factor_of


def setup_inputs(seed: int = 0) -> dict:
    streams_of = jax.random.split(jax.random.key(seed), 4)
    return {
        "right_side": draw_right_side(jax.random.fold_in(streams_of[3], 71), 0),
        "center": jnp.clip(4.0 + 2.0 * jax.random.uniform(streams_of[1], (NX, NY), jnp.float32) ** level_of(streams_of[1], (NX, NY), ((0, 8), (1, 4)), -0.2, 0.2), 4.0, 6.0),
        "couplings": jnp.clip(jnp.exp(math.log(1.0) - 2.3025851 * jax.random.uniform(streams_of[2], (4, NX, NY), jnp.float32) ** level_of(streams_of[2], (4, NX, NY), ((1, 8), (2, 4)), -0.2, 0.2)), 0.1, 1.0),
    }


def stencil(padded, shifted, couplings):
    middle = padded[:, 1:-1, 1:-1]
    nearby = couplings[0] * padded[:, :-2, 1:-1] + couplings[1] * padded[:, 2:, 1:-1]
    nearby = nearby + couplings[2] * padded[:, 1:-1, :-2]
    nearby = nearby + couplings[3] * padded[:, 1:-1, 2:]
    return shifted * middle - nearby

def cholesky_upper(gram_matrix):
    order = gram_matrix.shape[0]
    positions = jnp.arange(order, dtype=jnp.int32)

    def column_step(index, lower):
        picker = (positions == index).astype(gram_matrix.dtype)
        row_vals = jnp.dot(picker, lower, precision=lax.Precision.HIGHEST)
        remain = jnp.dot(gram_matrix, picker, precision=lax.Precision.HIGHEST) - jnp.dot(lower, row_vals, precision=lax.Precision.HIGHEST)
        pivot = jnp.sqrt(jnp.sum(remain * picker))
        column = jnp.where(positions >= index, remain / pivot, jnp.zeros_like(remain))
        return lower + column[:, None] * picker[None, :]
    lower = lax.fori_loop(0, order, column_step, jnp.zeros_like(gram_matrix))
    return lower.T

def upper_inverse(upper_factor):
    order = upper_factor.shape[0]
    positions = jnp.arange(order, dtype=jnp.int32)

    def row_step(count, inverse):
        index = order - 1 - count
        picker = (positions == index).astype(upper_factor.dtype)
        row_vals = jnp.dot(picker, upper_factor, precision=lax.Precision.HIGHEST)
        pivot = jnp.sum(row_vals * picker)
        solved = (picker - jnp.dot(row_vals, inverse, precision=lax.Precision.HIGHEST)) / pivot
        return inverse + picker[:, None] * solved[None, :]
    return lax.fori_loop(0, order, row_step, jnp.zeros_like(upper_factor))

def triangle_pair(gram_matrix):
    upper_factor = cholesky_upper(gram_matrix)
    return (upper_factor, upper_inverse(upper_factor))

def reference(right_side, center, couplings):
    shifted = center - 5.0
    blocks = [right_side]
    for power in range(S):
        padded = jnp.pad(blocks[-1], ((0, 0), (1, 1), (1, 1)))
        blocks.append(stencil(padded, shifted, couplings))
    basis = jnp.concatenate(blocks, 0).reshape(COLS, NX * NY)
    gram_one = jnp.dot(basis, basis.T, precision=lax.Precision.HIGHEST)
    upper_one, inverse_one = triangle_pair(gram_one)
    first_pass = jnp.dot(inverse_one.T, basis, precision=lax.Precision.HIGHEST)
    gram_two = jnp.dot(first_pass, first_pass.T, precision=lax.Precision.HIGHEST)
    upper_two, inverse_two = triangle_pair(gram_two)
    ortho = jnp.dot(inverse_two.T, first_pass, precision=lax.Precision.HIGHEST)
    upper_factor = jnp.dot(upper_two, upper_one, precision=lax.Precision.HIGHEST)
    norm_scale = math.sqrt(NX * NY)
    return ((ortho * norm_scale).reshape(COLS, NX, NY), upper_factor / norm_scale)
```

```python
import functools
import math

import jax
import jax.numpy as jnp
from jax import lax
from jax.experimental import pallas as pl
from jax.experimental.pallas import tpu as pltpu
from jax.sharding import PartitionSpec as P

S = 4
B = 16
COLS = B * (S + 1)
F32 = jnp.float32
BF16 = jnp.bfloat16
MESH = pl.DeviceIdType.MESH
VMEM_LIMIT = 56 * 1024 * 1024


def split(x, count):
    parts = []
    for _ in range(count - 1):
        part = x.astype(BF16)
        parts.append(part)
        x = x - part.astype(F32)
    parts.append(x.astype(BF16))
    return parts


def dot(a, b):
    return jnp.dot(a, b, preferred_element_type=F32)


def dot_nt(a, b):
    return lax.dot_general(a, b, (((1,), (1,)), ((), ())), preferred_element_type=F32)


def exchange(cells, axis, dim, width):
    count = lax.axis_size(axis)
    ends = count - 1
    size = cells.shape[dim]
    head = lax.slice_in_dim(cells, 0, width, axis=dim)
    tail = lax.slice_in_dim(cells, size - width, size, axis=dim)
    before = lax.ppermute(tail, axis, [(i, i + 1) for i in range(ends)])
    after = lax.ppermute(head, axis, [(i + 1, i) for i in range(ends)])
    return before, after


def powers_kernel(rows, cols, chunk, padded, basis, gram, held, acc, levels):
    step = pl.program_id(0)

    def apply(power, r):
        if power == 1:
            def src(i):
                return padded[i, 0:B, :]
        else:
            def src(i):
                return levels[(power - 1) % 2, i]
        here = src(r)
        width = here.shape[1]

        def coef(j):
            return padded[r, B + j : B + j + 1, :]

        near = coef(1) * src(r - 1) + coef(2) * src(r + 1)
        near = near + coef(3) * pltpu.roll(here, 1, 1)
        near = near + coef(4) * pltpu.roll(here, width - 1, 1)
        return coef(0) * here - near

    @pl.when(step == 0)
    def _():
        acc[...] = jnp.zeros_like(acc)

        def copy_row(r, carry):
            held[r, 0:B, :] = padded[r + S, 0:B, 0:cols]
            return carry

        lax.fori_loop(0, rows, copy_row, 0, unroll=4)
        for power in range(1, S + 1):
            for r in list(range(power, S)) + list(range(rows + S, rows + 2 * S - power)):
                levels[power % 2, r] = apply(power, r)

            def row(r, carry):
                out = apply(power, r + S)
                if power < S:
                    levels[power % 2, r + S] = out
                held[r, B * power : B * power + B, :] = out[:, 0:cols]
                return carry

            lax.fori_loop(0, rows, row, 0, unroll=4)

    basis[...] = held[pl.ds(step * chunk, chunk)]
    part = None
    for j in range(0, chunk, 4):
        wide = jnp.concatenate([held[step * chunk + j + i] for i in range(4)], axis=1)
        stack = jnp.concatenate(split(wide, 3), axis=0)
        add = dot_nt(stack, stack)
        part = add if part is None else part + add
    acc[...] += part

    @pl.when(step == pl.num_programs(0) - 1)
    def _():
        a = acc[...]
        c = COLS

        def block(i, j):
            return a[i * c : i * c + c, j * c : j * c + c]

        small = block(0, 2) + block(2, 0) + block(1, 1)
        total = block(0, 0) + ((block(0, 1) + block(1, 0)) + small)
        gram[...] = jnp.zeros_like(gram)
        gram[0:c, 0:c] = total


def powers(padded, rows, cols, pad_rows):
    chunk = 8
    return pl.pallas_call(
        functools.partial(powers_kernel, rows, cols, chunk),
        grid=(rows // chunk,),
        in_specs=[pl.BlockSpec(padded.shape, lambda i: (0, 0, 0))],
        out_specs=[
            pl.BlockSpec((chunk, COLS, cols), lambda i: (i, 0, 0)),
            pl.BlockSpec((pad_rows, 128), lambda i: (0, 0)),
        ],
        out_shape=[
            jax.ShapeDtypeStruct((rows, COLS, cols), F32),
            jax.ShapeDtypeStruct((pad_rows, 128), F32),
        ],
        scratch_shapes=[
            pltpu.VMEM((rows, COLS, cols), F32),
            pltpu.VMEM((3 * COLS, 3 * COLS), F32),
            pltpu.VMEM((2, padded.shape[0], B, padded.shape[2]), F32),
        ],
        compiler_params=pltpu.CompilerParams(vmem_limit_bytes=VMEM_LIMIT),
        name="powers",
    )(padded)


def total_kernel(nx, ny, piece, x_ref, out_ref, got_row, got_col, send, r1, r2, r3):
    gx, gy = lax.axis_index("gx"), lax.axis_index("gy")
    barrier = pltpu.get_barrier_semaphore()
    rows = [(gx, lax.rem(gy + d, ny)) for d in range(1, ny)]
    columns = [(lax.rem(gx + d, nx), gy) for d in range(1, nx)]
    for peer in rows + columns:
        pl.semaphore_signal(barrier, inc=1, device_id=peer, device_id_type=MESH)
    pl.semaphore_wait(barrier, len(rows) + len(columns))

    def push(src, dst, index, sem, peer):
        copy = pltpu.make_async_remote_copy(
            src_ref=src, dst_ref=dst, send_sem=send.at[index], recv_sem=sem,
            device_id=peer, device_id_type=MESH,
        )
        copy.start()
        return copy

    def part(i):
        return pl.ds(pl.multiple_of(i * piece, 8), piece)

    copies = [
        push(x_ref.at[part(peer[1])], got_row.at[gy], i, r1.at[i], peer)
        for i, peer in enumerate(rows)
    ]
    got_row[gy] = x_ref[part(gy)]
    for copy in copies:
        copy.wait()
    held = got_row[0]
    for i in range(1, ny):
        held = held + got_row[i]
    got_col[gx] = held
    copies = [
        push(got_col.at[gx], got_col.at[gx], i, r2.at[i], peer) for i, peer in enumerate(columns)
    ]
    for copy in copies:
        copy.wait()
    held = got_col[0]
    for i in range(1, nx):
        held = held + got_col[i]
    out_ref[part(gy)] = held
    copies = [
        push(out_ref.at[part(gy)], out_ref.at[part(gy)], i, r3.at[i], peer)
        for i, peer in enumerate(rows)
    ]
    for copy in copies:
        copy.wait()


def total(x, nx, ny, ident):
    piece = x.shape[0] // ny
    most = max(nx, ny) - 1
    return pl.pallas_call(
        functools.partial(total_kernel, nx, ny, piece),
        in_specs=[pl.BlockSpec(memory_space=pltpu.VMEM)],
        out_specs=pl.BlockSpec(memory_space=pltpu.VMEM),
        out_shape=jax.ShapeDtypeStruct(x.shape, F32),
        scratch_shapes=[
            pltpu.VMEM((ny, piece, 128), F32),
            pltpu.VMEM((nx, piece, 128), F32),
            pltpu.SemaphoreType.DMA((most,)),
            pltpu.SemaphoreType.DMA((max(ny - 1, 1),)),
            pltpu.SemaphoreType.DMA((max(nx - 1, 1),)),
            pltpu.SemaphoreType.DMA((max(ny - 1, 1),)),
        ],
        compiler_params=pltpu.CompilerParams(collective_id=ident, has_side_effects=True),
        name="total",
    )(x)


def eliminate(gram):
    c = COLS
    row_id = lax.broadcasted_iota(jnp.int32, (c, 128), 0)
    lane_id = lax.broadcasted_iota(jnp.int32, (c, 128), 1)
    work = jnp.concatenate([gram, (row_id == lane_id).astype(F32)], axis=1)
    tiles = [work[8 * t : 8 * t + 8] for t in range(c // 8)]
    sub = lax.broadcasted_iota(jnp.int32, (8, 1), 0)
    for k in range(c):
        t0, s0 = divmod(k, 8)
        row = tiles[t0][s0 : s0 + 1]
        pivot = row[:, k : k + 1]
        scale = 1.0 / jnp.sqrt(pivot)
        row = row * scale
        for t in range(t0, c // 8):
            mult = tiles[t][:, k : k + 1] * scale
            if t == t0:
                mult = jnp.where(sub > s0, mult, 0.0)
                tiles[t] = jnp.where(sub == s0, row, tiles[t] - mult * row)
            else:
                tiles[t] = tiles[t] - mult * row
    done = jnp.concatenate(tiles, axis=0)
    upper = jnp.where(lane_id >= row_id, done[:, 0:128], 0.0)
    return upper, done[:, 128:256]


def spread(parts):
    wide = None
    for i, part in enumerate(parts):
        one = jnp.concatenate([part.astype(F32), jnp.zeros_like(part, F32)], axis=1)
        if i:
            one = pltpu.roll(one, COLS * i, 1)
        wide = one if wide is None else wide + one
    return wide.astype(BF16)


def first_kernel(chunk, gram, basis, upper_ref, high, low, gram_out, left, acc):
    step = pl.program_id(0)

    @pl.when(step == 0)
    def _():
        acc[...] = jnp.zeros_like(acc)
        upper, inverse = eliminate(gram[0:COLS, :])
        upper_ref[...] = upper
        a, b, c = split(inverse, 3)
        left[0] = spread([a, b, a])
        left[1] = spread([c, b, a])

    pad = jnp.zeros((256 - 3 * COLS, basis.shape[2]), BF16)
    part = None
    for j in range(chunk):
        a, b, c = split(basis[j], 3)
        q = dot(left[0], jnp.concatenate([a, a, b, pad], axis=0))
        q = q + dot(left[1], jnp.concatenate([a, b, c, pad], axis=0))
        hi, lo = split(q, 2)
        high[j] = hi
        low[j] = lo
        stack = jnp.concatenate([hi, lo], axis=0)
        add = dot_nt(stack, stack)
        part = add if part is None else part + add
    acc[...] += part

    @pl.when(step == pl.num_programs(0) - 1)
    def _():
        c = COLS
        a = acc[...]
        gram_out[...] = jnp.zeros_like(gram_out)
        gram_out[0:c, 0:c] = a[0:c, 0:c] + (
            (a[0:c, c : 2 * c] + a[c : 2 * c, 0:c]) + a[c : 2 * c, c : 2 * c]
        )


def first(gram, basis):
    rows, _, cols = basis.shape
    chunk = 8
    return pl.pallas_call(
        functools.partial(first_kernel, chunk),
        grid=(rows // chunk,),
        in_specs=[
            pl.BlockSpec(gram.shape, lambda i: (0, 0)),
            pl.BlockSpec((chunk, COLS, cols), lambda i: (i, 0, 0)),
        ],
        out_specs=[
            pl.BlockSpec((COLS, 128), lambda i: (0, 0)),
            pl.BlockSpec((chunk, COLS, cols), lambda i: (i, 0, 0)),
            pl.BlockSpec((chunk, COLS, cols), lambda i: (i, 0, 0)),
            pl.BlockSpec(gram.shape, lambda i: (0, 0)),
        ],
        out_shape=[
            jax.ShapeDtypeStruct((COLS, 128), F32),
            jax.ShapeDtypeStruct((rows, COLS, cols), BF16),
            jax.ShapeDtypeStruct((rows, COLS, cols), BF16),
            jax.ShapeDtypeStruct(gram.shape, F32),
        ],
        scratch_shapes=[
            pltpu.VMEM((2, COLS, 256), BF16),
            pltpu.VMEM((2 * COLS, 2 * COLS), F32),
        ],
        compiler_params=pltpu.CompilerParams(vmem_limit_bytes=VMEM_LIMIT),
        name="first",
    )(gram, basis)


def second_kernel(chunk, norm, gram, upper_one, high, low, q_ref, r_ref, left):
    step = pl.program_id(0)

    @pl.when(step == 0)
    def _():
        upper, inverse = eliminate(gram[0:COLS, :])
        full = jnp.dot(
            upper[:, 0:COLS], upper_one[...], precision=lax.Precision.HIGHEST,
            preferred_element_type=F32,
        )
        r_ref[...] = full[:, 0:COLS] / norm
        a, b = split(inverse * norm, 2)
        left[...] = spread([a, b, a])

    pad = jnp.zeros((256 - 3 * COLS, high.shape[2]), BF16)
    out = []
    for j in range(chunk):
        hi, lo = high[j], low[j]
        out.append(dot(left[...], jnp.concatenate([hi, hi, lo, pad], axis=0)))
    q_ref[...] = jnp.swapaxes(jnp.stack(out, 0), 0, 1)


def second(gram, upper_one, high, low, norm):
    rows, _, cols = high.shape
    chunk = 8
    return pl.pallas_call(
        functools.partial(second_kernel, chunk, norm),
        grid=(rows // chunk,),
        in_specs=[
            pl.BlockSpec(gram.shape, lambda i: (0, 0)),
            pl.BlockSpec(upper_one.shape, lambda i: (0, 0)),
            pl.BlockSpec((chunk, COLS, cols), lambda i: (i, 0, 0)),
            pl.BlockSpec((chunk, COLS, cols), lambda i: (i, 0, 0)),
        ],
        out_specs=[
            pl.BlockSpec((COLS, chunk, cols), lambda i: (0, i, 0)),
            pl.BlockSpec((COLS, COLS), lambda i: (0, 0)),
        ],
        out_shape=[
            jax.ShapeDtypeStruct((COLS, rows, cols), F32),
            jax.ShapeDtypeStruct((COLS, COLS), F32),
        ],
        scratch_shapes=[pltpu.VMEM((COLS, 256), BF16)],
        compiler_params=pltpu.CompilerParams(vmem_limit_bytes=VMEM_LIMIT),
        name="second",
    )(gram, upper_one, high, low)


def on_device(nx, ny, right_side, center, couplings):
    rows, cols = center.shape
    norm = math.sqrt(rows * cols * nx * ny)
    fields = jnp.concatenate(
        [right_side, (center - 5.0)[None], couplings, jnp.zeros((3, rows, cols), F32)], 0
    )
    fields = jnp.swapaxes(fields, 0, 1)
    up, down = exchange(fields, "gx", 0, S)
    fields = jnp.concatenate([up, fields, down], 0)
    left, right = exchange(fields, "gy", 2, S)
    gap = jnp.zeros(fields.shape[:2] + (128 - 2 * S,), F32)
    padded = jnp.concatenate([fields, right, gap, left], 2)

    pad_rows = -(-COLS // (8 * ny)) * 8 * ny
    basis, gram = powers(padded, rows, cols, pad_rows)
    gram = total(gram, nx, ny, 1)
    upper_one, high, low, gram = first(gram, basis)
    gram = total(gram, nx, ny, 1)
    return second(gram, upper_one, high, low, norm)


def solution(mesh):
    placed = (P(None, "gx", "gy"), P("gx", "gy"), P(None, "gx", "gy"))
    return jax.shard_map(
        functools.partial(on_device, mesh.shape["gx"], mesh.shape["gy"]),
        mesh=mesh, in_specs=placed, out_specs=(P(None, "gx", "gy"), P()), check_vma=False,
    )
```

```python
import functools
import math

import jax
import jax.numpy as jnp
from jax import lax
from jax.experimental import pallas as pl
from jax.experimental.pallas import tpu as pltpu
from jax.sharding import PartitionSpec as P

S = 4
B = 16
COLS = B * (S + 1)
F32 = jnp.float32
BF16 = jnp.bfloat16
MESH = pl.DeviceIdType.MESH
VMEM_LIMIT = 56 * 1024 * 1024


def split(x, count):
    parts = []
    for _ in range(count - 1):
        part = x.astype(BF16)
        parts.append(part)
        x = x - part.astype(F32)
    parts.append(x.astype(BF16))
    return parts


def dot(a, b):
    return jnp.dot(a, b, preferred_element_type=F32)


def dot_nt(a, b):
    return lax.dot_general(a, b, (((1,), (1,)), ((), ())), preferred_element_type=F32)


FIELDS = B + 8
SIDES = [(-1, 0), (1, 0), (0, -1), (0, 1), (-1, -1), (-1, 1), (1, -1), (1, 1)]


def halo_kernel(nx, ny, right, center, couplings, out, packs, sides, corners, send, recv):
    gx, gy = lax.axis_index("gx"), lax.axis_index("gy")
    rows, cols = center.shape
    last = cols - 128

    def there(dx, dy):
        ok = None
        for test in ([gx > 0] if dx < 0 else [gx < nx - 1] if dx > 0 else []) + (
            [gy > 0] if dy < 0 else [gy < ny - 1] if dy > 0 else []
        ):
            ok = test if ok is None else jnp.logical_and(ok, test)
        return ok

    def device(dx, dy):
        return (lax.rem(gx + dx + nx, nx), lax.rem(gy + dy + ny, ny))

    barrier = pltpu.get_barrier_semaphore()
    for side in SIDES:
        @pl.when(there(*side))
        def _():
            pl.semaphore_signal(barrier, inc=1, device_id=device(*side), device_id_type=MESH)

    lane = lax.broadcasted_iota(jnp.int32, (FIELDS, 128), 1)
    per = 128 // S
    groups = rows // per
    for g in range(rows // 8):
        cut = pl.ds(8 * g, 8)
        fields = jnp.concatenate(
            [
                right[:, cut, :],
                (center[cut, :] - 5.0)[None],
                couplings[:, cut, :],
                jnp.zeros((FIELDS - B - 5, 8, cols), F32),
            ],
            axis=0,
        )
        out[S + 8 * g : S + 8 * g + 8, :, 0:cols] = jnp.swapaxes(fields, 0, 1)
    for g in range(groups):
        left = jnp.zeros((FIELDS, 128), F32)
        far = jnp.zeros((FIELDS, 128), F32)
        for j in range(per):
            r = S + g * per + j
            here = (lane >= S * j) & (lane < S * j + S)
            a = out[r, :, 0:128]
            z = out[r, :, last : last + 128]
            left = jnp.where(here, pltpu.roll(a, S * j, 1) if j else a, left)
            shift = (S * j + S) % 128
            far = jnp.where(here, pltpu.roll(z, shift, 1) if shift else z, far)
        packs[0, g] = left
        packs[1, g] = far

    near_x = (gx > 0).astype(jnp.int32) + (gx < nx - 1).astype(jnp.int32)
    near_y = (gy > 0).astype(jnp.int32) + (gy < ny - 1).astype(jnp.int32)
    pl.semaphore_wait(barrier, (1 + near_x) * (1 + near_y) - 1)

    ends = groups - 1
    core = pl.ds(0, cols)
    ways = [
        (out.at[pl.ds(S, S), :, core], out.at[pl.ds(rows + S, S), :, core]),
        (out.at[pl.ds(rows, S), :, core], out.at[pl.ds(0, S), :, core]),
        (packs.at[0], sides.at[1]),
        (packs.at[1], sides.at[0]),
        (packs.at[0, 0], corners.at[3]),
        (packs.at[1, 0], corners.at[2]),
        (packs.at[0, ends], corners.at[1]),
        (packs.at[1, ends], corners.at[0]),
    ]
    copies = [
        pltpu.make_async_remote_copy(
            src_ref=src, dst_ref=dst, send_sem=send.at[i], recv_sem=recv.at[i],
            device_id=device(*SIDES[i]), device_id_type=MESH,
        )
        for i, (src, dst) in enumerate(ways)
    ]
    for i, side in enumerate(SIDES):
        @pl.when(there(*side))
        def _():
            copies[i].start()

    for i, (dx, dy) in enumerate(SIDES):
        dst = ways[i][1]
        came = there(-dx, -dy)

        @pl.when(jnp.logical_not(came))
        def _():
            dst[...] = jnp.zeros(dst.shape, F32)

        @pl.when(came)
        def _():
            copies[i].wait_recv()

    def halo(near, far, j):
        a = pltpu.roll(far, (128 - S * j) % 128, 1) if j else far
        shift = (128 - S - S * j) % 128
        z = pltpu.roll(near, shift, 1) if shift else near
        return jnp.where(lane < S, a, jnp.where(lane >= 128 - S, z, 0.0))

    tail = slice(cols, cols + 128)
    for g in range(groups):
        near, far = sides[0, g], sides[1, g]
        for j in range(per):
            out[S + g * per + j, :, tail] = halo(near, far, j)
    for i in range(S):
        out[i, :, tail] = halo(corners[0], corners[1], per - S + i)
        out[rows + S + i, :, tail] = halo(corners[2], corners[3], i)

    for i, side in enumerate(SIDES):
        @pl.when(there(*side))
        def _():
            copies[i].wait_send()


def halo_fields(nx, ny, right_side, center, couplings):
    rows, cols = center.shape
    groups = rows * S // 128
    return pl.pallas_call(
        functools.partial(halo_kernel, nx, ny),
        in_specs=[pl.BlockSpec(memory_space=pltpu.VMEM)] * 3,
        out_specs=pl.BlockSpec(memory_space=pltpu.VMEM),
        out_shape=jax.ShapeDtypeStruct((rows + 2 * S, FIELDS, cols + 128), F32),
        scratch_shapes=[
            pltpu.VMEM((2, groups, FIELDS, 128), F32),
            pltpu.VMEM((2, groups, FIELDS, 128), F32),
            pltpu.VMEM((4, FIELDS, 128), F32),
            pltpu.SemaphoreType.DMA((8,)),
            pltpu.SemaphoreType.DMA((8,)),
        ],
        compiler_params=pltpu.CompilerParams(
            collective_id=2, has_side_effects=True, vmem_limit_bytes=VMEM_LIMIT
        ),
        name="halo",
    )(right_side, center, couplings)


def powers_kernel(rows, cols, chunk, padded, basis, gram, held, acc, levels):
    step = pl.program_id(0)

    def apply(power, r):
        if power == 1:
            def src(i):
                return padded[i, 0:B, :]
        else:
            def src(i):
                return levels[(power - 1) % 2, i]
        here = src(r)
        width = here.shape[1]

        def coef(j):
            return padded[r, B + j : B + j + 1, :]

        near = coef(1) * src(r - 1) + coef(2) * src(r + 1)
        near = near + coef(3) * pltpu.roll(here, 1, 1)
        near = near + coef(4) * pltpu.roll(here, width - 1, 1)
        return coef(0) * here - near

    @pl.when(step == 0)
    def _():
        acc[...] = jnp.zeros_like(acc)

        def copy_row(r, carry):
            held[r, 0:B, :] = padded[r + S, 0:B, 0:cols]
            return carry

        lax.fori_loop(0, rows, copy_row, 0, unroll=4)
        for power in range(1, S + 1):
            for r in list(range(power, S)) + list(range(rows + S, rows + 2 * S - power)):
                levels[power % 2, r] = apply(power, r)

            def row(r, carry):
                out = apply(power, r + S)
                if power < S:
                    levels[power % 2, r + S] = out
                held[r, B * power : B * power + B, :] = out[:, 0:cols]
                return carry

            lax.fori_loop(0, rows, row, 0, unroll=4)

    basis[...] = held[pl.ds(step * chunk, chunk)]
    part = None
    for j in range(0, chunk, 4):
        wide = jnp.concatenate([held[step * chunk + j + i] for i in range(4)], axis=1)
        stack = jnp.concatenate(split(wide, 3), axis=0)
        add = dot_nt(stack, stack)
        part = add if part is None else part + add
    acc[...] += part

    @pl.when(step == pl.num_programs(0) - 1)
    def _():
        a = acc[...]
        c = COLS

        def block(i, j):
            return a[i * c : i * c + c, j * c : j * c + c]

        small = block(0, 2) + block(2, 0) + block(1, 1)
        total = block(0, 0) + ((block(0, 1) + block(1, 0)) + small)
        gram[...] = jnp.zeros_like(gram)
        gram[0:c, 0:c] = total


def powers(padded, rows, cols, pad_rows):
    chunk = 8
    return pl.pallas_call(
        functools.partial(powers_kernel, rows, cols, chunk),
        grid=(rows // chunk,),
        in_specs=[pl.BlockSpec(padded.shape, lambda i: (0, 0, 0))],
        out_specs=[
            pl.BlockSpec((chunk, COLS, cols), lambda i: (i, 0, 0)),
            pl.BlockSpec((pad_rows, 128), lambda i: (0, 0)),
        ],
        out_shape=[
            jax.ShapeDtypeStruct((rows, COLS, cols), F32),
            jax.ShapeDtypeStruct((pad_rows, 128), F32),
        ],
        scratch_shapes=[
            pltpu.VMEM((rows, COLS, cols), F32),
            pltpu.VMEM((3 * COLS, 3 * COLS), F32),
            pltpu.VMEM((2, padded.shape[0], B, padded.shape[2]), F32),
        ],
        compiler_params=pltpu.CompilerParams(vmem_limit_bytes=VMEM_LIMIT),
        name="powers",
    )(padded)


def total_kernel(nx, ny, piece, x_ref, out_ref, got_row, got_col, send, r1, r2, r3):
    gx, gy = lax.axis_index("gx"), lax.axis_index("gy")
    barrier = pltpu.get_barrier_semaphore()
    rows = [(gx, lax.rem(gy + d, ny)) for d in range(1, ny)]
    columns = [(lax.rem(gx + d, nx), gy) for d in range(1, nx)]
    for peer in rows + columns:
        pl.semaphore_signal(barrier, inc=1, device_id=peer, device_id_type=MESH)
    pl.semaphore_wait(barrier, len(rows) + len(columns))

    def push(src, dst, index, sem, peer):
        copy = pltpu.make_async_remote_copy(
            src_ref=src, dst_ref=dst, send_sem=send.at[index], recv_sem=sem,
            device_id=peer, device_id_type=MESH,
        )
        copy.start()
        return copy

    def part(i):
        return pl.ds(pl.multiple_of(i * piece, 8), piece)

    copies = [
        push(x_ref.at[part(peer[1])], got_row.at[gy], i, r1.at[i], peer)
        for i, peer in enumerate(rows)
    ]
    got_row[gy] = x_ref[part(gy)]
    for copy in copies:
        copy.wait()
    held = got_row[0]
    for i in range(1, ny):
        held = held + got_row[i]
    got_col[gx] = held
    copies = [
        push(got_col.at[gx], got_col.at[gx], i, r2.at[i], peer) for i, peer in enumerate(columns)
    ]
    for copy in copies:
        copy.wait()
    held = got_col[0]
    for i in range(1, nx):
        held = held + got_col[i]
    out_ref[part(gy)] = held
    copies = [
        push(out_ref.at[part(gy)], out_ref.at[part(gy)], i, r3.at[i], peer)
        for i, peer in enumerate(rows)
    ]
    for copy in copies:
        copy.wait()


def total(x, nx, ny, ident):
    piece = x.shape[0] // ny
    most = max(nx, ny) - 1
    return pl.pallas_call(
        functools.partial(total_kernel, nx, ny, piece),
        in_specs=[pl.BlockSpec(memory_space=pltpu.VMEM)],
        out_specs=pl.BlockSpec(memory_space=pltpu.VMEM),
        out_shape=jax.ShapeDtypeStruct(x.shape, F32),
        scratch_shapes=[
            pltpu.VMEM((ny, piece, 128), F32),
            pltpu.VMEM((nx, piece, 128), F32),
            pltpu.SemaphoreType.DMA((most,)),
            pltpu.SemaphoreType.DMA((max(ny - 1, 1),)),
            pltpu.SemaphoreType.DMA((max(nx - 1, 1),)),
            pltpu.SemaphoreType.DMA((max(ny - 1, 1),)),
        ],
        compiler_params=pltpu.CompilerParams(collective_id=ident, has_side_effects=True),
        name="total",
    )(x)


def eliminate(gram):
    c = COLS
    row_id = lax.broadcasted_iota(jnp.int32, (c, 128), 0)
    lane_id = lax.broadcasted_iota(jnp.int32, (c, 128), 1)
    eye = (row_id == lane_id).astype(F32)
    upper = [gram[8 * t : 8 * t + 8] for t in range(c // 8)]
    lower = [eye[8 * t : 8 * t + 8] for t in range(c // 8)]
    sub = lax.broadcasted_iota(jnp.int32, (8, 128), 0)
    scales = []
    for b in range(c // 8):
        later = range(b, c // 8)
        columns = {
            t: [
                jnp.broadcast_to(upper[t][:, 8 * b + j : 8 * b + j + 1], (8, 128))
                for j in range(8)
            ]
            for t in later
        }
        scale = jnp.zeros((8, 128), F32)
        for j in range(8):
            heads = [columns[b][i][j : j + 1] for i in range(8)]
            inv = 1.0 / heads[j]
            scale = jnp.where(sub == j, heads[j], scale)
            row_u, row_l = upper[b][j : j + 1], lower[b][j : j + 1]
            for t in later:
                mult = columns[t][j] * inv
                if t == b:
                    mult = jnp.where(sub > j, mult, 0.0)
                for i in range(j + 1, 8):
                    columns[t][i] = columns[t][i] - mult * heads[i]
                upper[t] = upper[t] - mult * row_u
                lower[t] = lower[t] - mult * row_l
        scales.append(scale)
    scale = 1.0 / jnp.sqrt(jnp.concatenate(scales, axis=0))
    up = jnp.concatenate(upper, axis=0) * scale
    return jnp.where(lane_id >= row_id, up, 0.0), jnp.concatenate(lower, axis=0) * scale


def spread(parts):
    wide = None
    for i, part in enumerate(parts):
        one = jnp.concatenate([part.astype(F32), jnp.zeros_like(part, F32)], axis=1)
        if i:
            one = pltpu.roll(one, COLS * i, 1)
        wide = one if wide is None else wide + one
    return wide.astype(BF16)


def first_kernel(chunk, gram, basis, upper_ref, high, low, gram_out, left, acc):
    step = pl.program_id(0)

    @pl.when(step == 0)
    def _():
        acc[...] = jnp.zeros_like(acc)
        upper, inverse = eliminate(gram[0:COLS, :])
        upper_ref[...] = upper
        a, b, c = split(inverse, 3)
        left[0] = spread([a, b, a])
        left[1] = spread([c, b, a])

    pad = jnp.zeros((256 - 3 * COLS, basis.shape[2]), BF16)
    part = None
    for j in range(chunk):
        a, b, c = split(basis[j], 3)
        q = dot(left[0], jnp.concatenate([a, a, b, pad], axis=0))
        q = q + dot(left[1], jnp.concatenate([a, b, c, pad], axis=0))
        hi, lo = split(q, 2)
        high[j] = hi
        low[j] = lo
        stack = jnp.concatenate([hi, lo], axis=0)
        add = dot_nt(stack, stack)
        part = add if part is None else part + add
    acc[...] += part

    @pl.when(step == pl.num_programs(0) - 1)
    def _():
        c = COLS
        a = acc[...]
        gram_out[...] = jnp.zeros_like(gram_out)
        gram_out[0:c, 0:c] = a[0:c, 0:c] + (
            (a[0:c, c : 2 * c] + a[c : 2 * c, 0:c]) + a[c : 2 * c, c : 2 * c]
        )


def first(gram, basis):
    rows, _, cols = basis.shape
    chunk = 8
    return pl.pallas_call(
        functools.partial(first_kernel, chunk),
        grid=(rows // chunk,),
        in_specs=[
            pl.BlockSpec(gram.shape, lambda i: (0, 0)),
            pl.BlockSpec((chunk, COLS, cols), lambda i: (i, 0, 0)),
        ],
        out_specs=[
            pl.BlockSpec((COLS, 128), lambda i: (0, 0)),
            pl.BlockSpec((chunk, COLS, cols), lambda i: (i, 0, 0)),
            pl.BlockSpec((chunk, COLS, cols), lambda i: (i, 0, 0)),
            pl.BlockSpec(gram.shape, lambda i: (0, 0)),
        ],
        out_shape=[
            jax.ShapeDtypeStruct((COLS, 128), F32),
            jax.ShapeDtypeStruct((rows, COLS, cols), BF16),
            jax.ShapeDtypeStruct((rows, COLS, cols), BF16),
            jax.ShapeDtypeStruct(gram.shape, F32),
        ],
        scratch_shapes=[
            pltpu.VMEM((2, COLS, 256), BF16),
            pltpu.VMEM((2 * COLS, 2 * COLS), F32),
        ],
        compiler_params=pltpu.CompilerParams(vmem_limit_bytes=VMEM_LIMIT),
        name="first",
    )(gram, basis)


def second_kernel(chunk, norm, gram, upper_one, high, low, q_ref, r_ref, left):
    step = pl.program_id(0)

    @pl.when(step == 0)
    def _():
        upper, inverse = eliminate(gram[0:COLS, :])
        full = jnp.dot(
            upper[:, 0:COLS], upper_one[...], precision=lax.Precision.HIGHEST,
            preferred_element_type=F32,
        )
        r_ref[...] = full[:, 0:COLS] / norm
        a, b = split(inverse * norm, 2)
        left[...] = spread([a, b, a])

    pad = jnp.zeros((256 - 3 * COLS, high.shape[2]), BF16)
    out = []
    for j in range(chunk):
        hi, lo = high[j], low[j]
        out.append(dot(left[...], jnp.concatenate([hi, hi, lo, pad], axis=0)))
    q_ref[...] = jnp.swapaxes(jnp.stack(out, 0), 0, 1)


def second(gram, upper_one, high, low, norm):
    rows, _, cols = high.shape
    chunk = 8
    return pl.pallas_call(
        functools.partial(second_kernel, chunk, norm),
        grid=(rows // chunk,),
        in_specs=[
            pl.BlockSpec(gram.shape, lambda i: (0, 0)),
            pl.BlockSpec(upper_one.shape, lambda i: (0, 0)),
            pl.BlockSpec((chunk, COLS, cols), lambda i: (i, 0, 0)),
            pl.BlockSpec((chunk, COLS, cols), lambda i: (i, 0, 0)),
        ],
        out_specs=[
            pl.BlockSpec((COLS, chunk, cols), lambda i: (0, i, 0)),
            pl.BlockSpec((COLS, COLS), lambda i: (0, 0)),
        ],
        out_shape=[
            jax.ShapeDtypeStruct((COLS, rows, cols), F32),
            jax.ShapeDtypeStruct((COLS, COLS), F32),
        ],
        scratch_shapes=[pltpu.VMEM((COLS, 256), BF16)],
        compiler_params=pltpu.CompilerParams(vmem_limit_bytes=VMEM_LIMIT),
        name="second",
    )(gram, upper_one, high, low)


def on_device(nx, ny, right_side, center, couplings):
    rows, cols = center.shape
    norm = math.sqrt(rows * cols * nx * ny)
    padded = halo_fields(nx, ny, right_side, center, couplings)
    pad_rows = -(-COLS // (8 * ny)) * 8 * ny
    basis, gram = powers(padded, rows, cols, pad_rows)
    gram = total(gram, nx, ny, 1)
    upper_one, high, low, gram = first(gram, basis)
    gram = total(gram, nx, ny, 1)
    return second(gram, upper_one, high, low, norm)


def solution(mesh):
    placed = (P(None, "gx", "gy"), P("gx", "gy"), P(None, "gx", "gy"))
    return jax.shard_map(
        functools.partial(on_device, mesh.shape["gx"], mesh.shape["gy"]),
        mesh=mesh, in_specs=placed, out_specs=(P(None, "gx", "gy"), P()), check_vma=False,
    )
```

```python
import functools
import math

import jax
import jax.numpy as jnp
from jax import lax
from jax.experimental import pallas as pl
from jax.experimental.pallas import tpu as pltpu
from jax.sharding import PartitionSpec as P

S = 4
B = 16
COLS = B * (S + 1)
F32 = jnp.float32
BF16 = jnp.bfloat16
MESH = pl.DeviceIdType.MESH
VMEM_LIMIT = 56 * 1024 * 1024


def split(x, count):
    parts = []
    for _ in range(count - 1):
        part = x.astype(BF16)
        parts.append(part)
        x = x - part.astype(F32)
    parts.append(x.astype(BF16))
    return parts


def dot(a, b):
    return jnp.dot(a, b, preferred_element_type=F32)


def dot_nt(a, b):
    return lax.dot_general(a, b, (((1,), (1,)), ((), ())), preferred_element_type=F32)


FIELDS = B + 8
SIDES = [(-1, 0), (1, 0), (0, -1), (0, 1), (-1, -1), (-1, 1), (1, -1), (1, 1)]


def halo_kernel(nx, ny, right, center, couplings, out, packs, sides, corners, send, recv):
    gx, gy = lax.axis_index("gx"), lax.axis_index("gy")
    rows, cols = center.shape
    last = cols - 128

    def there(dx, dy):
        ok = None
        for test in ([gx > 0] if dx < 0 else [gx < nx - 1] if dx > 0 else []) + (
            [gy > 0] if dy < 0 else [gy < ny - 1] if dy > 0 else []
        ):
            ok = test if ok is None else jnp.logical_and(ok, test)
        return ok

    def device(dx, dy):
        return (lax.rem(gx + dx + nx, nx), lax.rem(gy + dy + ny, ny))

    barrier = pltpu.get_barrier_semaphore()
    for side in SIDES:
        @pl.when(there(*side))
        def _():
            pl.semaphore_signal(barrier, inc=1, device_id=device(*side), device_id_type=MESH)

    lane = lax.broadcasted_iota(jnp.int32, (FIELDS, 128), 1)
    per = 128 // S
    groups = rows // per
    for g in range(rows // 8):
        cut = pl.ds(8 * g, 8)
        fields = jnp.concatenate(
            [
                right[:, cut, :],
                (center[cut, :] - 5.0)[None],
                couplings[:, cut, :],
                jnp.zeros((FIELDS - B - 5, 8, cols), F32),
            ],
            axis=0,
        )
        out[S + 8 * g : S + 8 * g + 8, :, 0:cols] = jnp.swapaxes(fields, 0, 1)
    for g in range(groups):
        left = jnp.zeros((FIELDS, 128), F32)
        far = jnp.zeros((FIELDS, 128), F32)
        for j in range(per):
            r = S + g * per + j
            here = (lane >= S * j) & (lane < S * j + S)
            a = out[r, :, 0:128]
            z = out[r, :, last : last + 128]
            left = jnp.where(here, pltpu.roll(a, S * j, 1) if j else a, left)
            shift = (S * j + S) % 128
            far = jnp.where(here, pltpu.roll(z, shift, 1) if shift else z, far)
        packs[0, g] = left
        packs[1, g] = far

    near_x = (gx > 0).astype(jnp.int32) + (gx < nx - 1).astype(jnp.int32)
    near_y = (gy > 0).astype(jnp.int32) + (gy < ny - 1).astype(jnp.int32)
    pl.semaphore_wait(barrier, (1 + near_x) * (1 + near_y) - 1)

    ends = groups - 1
    core = pl.ds(0, cols)
    ways = [
        (out.at[pl.ds(S, S), :, core], out.at[pl.ds(rows + S, S), :, core]),
        (out.at[pl.ds(rows, S), :, core], out.at[pl.ds(0, S), :, core]),
        (packs.at[0], sides.at[1]),
        (packs.at[1], sides.at[0]),
        (packs.at[0, 0], corners.at[3]),
        (packs.at[1, 0], corners.at[2]),
        (packs.at[0, ends], corners.at[1]),
        (packs.at[1, ends], corners.at[0]),
    ]
    copies = [
        pltpu.make_async_remote_copy(
            src_ref=src, dst_ref=dst, send_sem=send.at[i], recv_sem=recv.at[i],
            device_id=device(*SIDES[i]), device_id_type=MESH,
        )
        for i, (src, dst) in enumerate(ways)
    ]
    for i, side in enumerate(SIDES):
        @pl.when(there(*side))
        def _():
            copies[i].start()

    for i, (dx, dy) in enumerate(SIDES):
        dst = ways[i][1]
        came = there(-dx, -dy)

        @pl.when(jnp.logical_not(came))
        def _():
            dst[...] = jnp.zeros(dst.shape, F32)

        @pl.when(came)
        def _():
            copies[i].wait_recv()

    def halo(near, far, j):
        a = pltpu.roll(far, (128 - S * j) % 128, 1) if j else far
        shift = (128 - S - S * j) % 128
        z = pltpu.roll(near, shift, 1) if shift else near
        return jnp.where(lane < S, a, jnp.where(lane >= 128 - S, z, 0.0))

    tail = slice(cols, cols + 128)
    for g in range(groups):
        near, far = sides[0, g], sides[1, g]
        for j in range(per):
            out[S + g * per + j, :, tail] = halo(near, far, j)
    for i in range(S):
        out[i, :, tail] = halo(corners[0], corners[1], per - S + i)
        out[rows + S + i, :, tail] = halo(corners[2], corners[3], i)

    for i, side in enumerate(SIDES):
        @pl.when(there(*side))
        def _():
            copies[i].wait_send()


def halo_fields(nx, ny, right_side, center, couplings):
    rows, cols = center.shape
    groups = rows * S // 128
    return pl.pallas_call(
        functools.partial(halo_kernel, nx, ny),
        in_specs=[pl.BlockSpec(memory_space=pltpu.VMEM)] * 3,
        out_specs=pl.BlockSpec(memory_space=pltpu.VMEM),
        out_shape=jax.ShapeDtypeStruct((rows + 2 * S, FIELDS, cols + 128), F32),
        scratch_shapes=[
            pltpu.VMEM((2, groups, FIELDS, 128), F32),
            pltpu.VMEM((2, groups, FIELDS, 128), F32),
            pltpu.VMEM((4, FIELDS, 128), F32),
            pltpu.SemaphoreType.DMA((8,)),
            pltpu.SemaphoreType.DMA((8,)),
        ],
        compiler_params=pltpu.CompilerParams(
            collective_id=2, has_side_effects=True, vmem_limit_bytes=VMEM_LIMIT
        ),
        name="halo",
    )(right_side, center, couplings)


class Total:
    def __init__(self, nx, ny):
        self.nx, self.ny = nx, ny
        self.pad_rows = -(-COLS // (8 * ny)) * 8 * ny
        self.piece = self.pad_rows // ny

    def scratch(self):
        nx, ny = self.nx, self.ny
        return [
            pltpu.VMEM((self.pad_rows, 128), F32),
            pltpu.VMEM((self.pad_rows, 128), F32),
            pltpu.VMEM((ny, self.piece, 128), F32),
            pltpu.VMEM((nx, self.piece, 128), F32),
            pltpu.SemaphoreType.DMA((max(nx, ny),)),
            pltpu.SemaphoreType.DMA((ny,)),
            pltpu.SemaphoreType.DMA((nx,)),
            pltpu.SemaphoreType.DMA((ny,)),
        ]

    def peers(self):
        nx, ny = self.nx, self.ny
        gx, gy = lax.axis_index("gx"), lax.axis_index("gy")
        rows = [(gx, lax.rem(gy + d, ny)) for d in range(1, ny)]
        columns = [(lax.rem(gx + d, nx), gy) for d in range(1, nx)]
        return gx, gy, rows, columns

    def greet(self):
        _, _, rows, columns = self.peers()
        barrier = pltpu.get_barrier_semaphore()
        for peer in rows + columns:
            pl.semaphore_signal(barrier, inc=1, device_id=peer, device_id_type=MESH)

    def run(self, scratch):
        x_ref, out_ref, got_row, got_col, send, r1, r2, r3 = scratch
        gx, gy, rows, columns = self.peers()
        pl.semaphore_wait(pltpu.get_barrier_semaphore(), len(rows) + len(columns))

        def push(src, dst, index, sem, peer):
            copy = pltpu.make_async_remote_copy(
                src_ref=src, dst_ref=dst, send_sem=send.at[index], recv_sem=sem,
                device_id=peer, device_id_type=MESH,
            )
            copy.start()
            return copy

        def part(i):
            return pl.ds(pl.multiple_of(i * self.piece, 8), self.piece)

        copies = [
            push(x_ref.at[part(peer[1])], got_row.at[gy], i, r1.at[i], peer)
            for i, peer in enumerate(rows)
        ]
        got_row[gy] = x_ref[part(gy)]
        for copy in copies:
            copy.wait()
        held = got_row[0]
        for i in range(1, self.ny):
            held = held + got_row[i]
        got_col[gx] = held
        copies = [
            push(got_col.at[gx], got_col.at[gx], i, r2.at[i], peer)
            for i, peer in enumerate(columns)
        ]
        for copy in copies:
            copy.wait()
        held = got_col[0]
        for i in range(1, self.nx):
            held = held + got_col[i]
        out_ref[part(gy)] = held
        copies = [
            push(out_ref.at[part(gy)], out_ref.at[part(gy)], i, r3.at[i], peer)
            for i, peer in enumerate(rows)
        ]
        for copy in copies:
            copy.wait()


def powers_kernel(total, rows, cols, chunk, padded, basis, gram, held, acc, levels, *scratch):
    step = pl.program_id(0)

    @pl.when(step == 0)
    def _():
        total.greet()

    def apply(power, r):
        if power == 1:
            def src(i):
                return padded[i, 0:B, :]
        else:
            def src(i):
                return levels[(power - 1) % 2, i]
        here = src(r)
        width = here.shape[1]

        def coef(j):
            return padded[r, B + j : B + j + 1, :]

        near = coef(1) * src(r - 1) + coef(2) * src(r + 1)
        near = near + coef(3) * pltpu.roll(here, 1, 1)
        near = near + coef(4) * pltpu.roll(here, width - 1, 1)
        return coef(0) * here - near

    @pl.when(step == 0)
    def _():
        acc[...] = jnp.zeros_like(acc)

        def copy_row(r, carry):
            held[r, 0:B, :] = padded[r + S, 0:B, 0:cols]
            return carry

        lax.fori_loop(0, rows, copy_row, 0, unroll=4)
        for power in range(1, S + 1):
            for r in list(range(power, S)) + list(range(rows + S, rows + 2 * S - power)):
                levels[power % 2, r] = apply(power, r)

            def row(r, carry):
                out = apply(power, r + S)
                if power < S:
                    levels[power % 2, r + S] = out
                held[r, B * power : B * power + B, :] = out[:, 0:cols]
                return carry

            lax.fori_loop(0, rows, row, 0, unroll=4)

    basis[...] = held[pl.ds(step * chunk, chunk)]
    part = None
    for j in range(0, chunk, 4):
        wide = jnp.concatenate([held[step * chunk + j + i] for i in range(4)], axis=1)
        stack = jnp.concatenate(split(wide, 3), axis=0)
        add = dot_nt(stack, stack)
        part = add if part is None else part + add
    acc[...] += part

    @pl.when(step == pl.num_programs(0) - 1)
    def _():
        a = acc[...]
        c = COLS

        def block(i, j):
            return a[i * c : i * c + c, j * c : j * c + c]

        small = block(0, 2) + block(2, 0) + block(1, 1)
        own = scratch[0]
        own[...] = jnp.zeros_like(own)
        own[0:c, 0:c] = block(0, 0) + ((block(0, 1) + block(1, 0)) + small)
        total.run(scratch)
        gram[...] = scratch[1][...]


def powers(total, padded, rows, cols):
    pad_rows = total.pad_rows
    chunk = 8
    return pl.pallas_call(
        functools.partial(powers_kernel, total, rows, cols, chunk),
        grid=(rows // chunk,),
        in_specs=[pl.BlockSpec(padded.shape, lambda i: (0, 0, 0))],
        out_specs=[
            pl.BlockSpec((chunk, COLS, cols), lambda i: (i, 0, 0)),
            pl.BlockSpec((pad_rows, 128), lambda i: (0, 0)),
        ],
        out_shape=[
            jax.ShapeDtypeStruct((rows, COLS, cols), F32),
            jax.ShapeDtypeStruct((pad_rows, 128), F32),
        ],
        scratch_shapes=[
            pltpu.VMEM((rows, COLS, cols), F32),
            pltpu.VMEM((3 * COLS, 3 * COLS), F32),
            pltpu.VMEM((2, padded.shape[0], B, padded.shape[2]), F32),
        ]
        + total.scratch(),
        compiler_params=pltpu.CompilerParams(
            collective_id=0, has_side_effects=True, vmem_limit_bytes=VMEM_LIMIT
        ),
        name="powers",
    )(padded)


def eliminate(gram):
    c = COLS
    row_id = lax.broadcasted_iota(jnp.int32, (c, 128), 0)
    lane_id = lax.broadcasted_iota(jnp.int32, (c, 128), 1)
    eye = (row_id == lane_id).astype(F32)
    upper = [gram[8 * t : 8 * t + 8] for t in range(c // 8)]
    lower = [eye[8 * t : 8 * t + 8] for t in range(c // 8)]
    sub = lax.broadcasted_iota(jnp.int32, (8, 128), 0)
    scales = []
    for b in range(c // 8):
        later = range(b, c // 8)
        columns = {
            t: [
                jnp.broadcast_to(upper[t][:, 8 * b + j : 8 * b + j + 1], (8, 128))
                for j in range(8)
            ]
            for t in later
        }
        scale = jnp.zeros((8, 128), F32)
        for j in range(8):
            heads = [columns[b][i][j : j + 1] for i in range(8)]
            inv = 1.0 / heads[j]
            inv = inv * (2.0 - heads[j] * inv)
            scale = jnp.where(sub == j, heads[j], scale)
            row_u, row_l = upper[b][j : j + 1], lower[b][j : j + 1]
            for t in later:
                mult = columns[t][j] * inv
                if t == b:
                    mult = jnp.where(sub > j, mult, 0.0)
                for i in range(j + 1, 8):
                    columns[t][i] = columns[t][i] - mult * heads[i]
                upper[t] = upper[t] - mult * row_u
                lower[t] = lower[t] - mult * row_l
        scales.append(scale)
    pivots = jnp.concatenate(scales, axis=0)
    scale = 1.0 / jnp.sqrt(pivots)
    scale = scale * (1.5 - 0.5 * (pivots * scale) * scale)
    up = jnp.concatenate(upper, axis=0) * scale
    return jnp.where(lane_id >= row_id, up, 0.0), jnp.concatenate(lower, axis=0) * scale


def spread(parts):
    wide = None
    for i, part in enumerate(parts):
        one = jnp.concatenate([part.astype(F32), jnp.zeros_like(part, F32)], axis=1)
        if i:
            one = pltpu.roll(one, COLS * i, 1)
        wide = one if wide is None else wide + one
    return wide.astype(BF16)


def first_kernel(total, chunk, gram, basis, upper_ref, high, low, gram_out, left, acc, *scratch):
    step = pl.program_id(0)

    @pl.when(step == 0)
    def _():
        total.greet()
        acc[...] = jnp.zeros_like(acc)
        upper, inverse = eliminate(gram[0:COLS, :])
        upper_ref[...] = upper
        a, b, c = split(inverse, 3)
        left[0] = spread([a, b, a])
        left[1] = spread([c, b, a])

    pad = jnp.zeros((256 - 3 * COLS, basis.shape[2]), BF16)
    part = None
    for j in range(chunk):
        a, b, c = split(basis[j], 3)
        q = dot(left[0], jnp.concatenate([a, a, b, pad], axis=0))
        q = q + dot(left[1], jnp.concatenate([a, b, c, pad], axis=0))
        hi, lo = split(q, 2)
        high[j] = hi
        low[j] = lo
        stack = jnp.concatenate([hi, lo], axis=0)
        add = dot_nt(stack, stack)
        part = add if part is None else part + add
    acc[...] += part

    @pl.when(step == pl.num_programs(0) - 1)
    def _():
        c = COLS
        a = acc[...]
        own = scratch[0]
        own[...] = jnp.zeros_like(own)
        own[0:c, 0:c] = a[0:c, 0:c] + (
            (a[0:c, c : 2 * c] + a[c : 2 * c, 0:c]) + a[c : 2 * c, c : 2 * c]
        )
        total.run(scratch)
        gram_out[...] = scratch[1][...]


def first(total, gram, basis):
    rows, _, cols = basis.shape
    chunk = 8
    return pl.pallas_call(
        functools.partial(first_kernel, total, chunk),
        grid=(rows // chunk,),
        in_specs=[
            pl.BlockSpec(gram.shape, lambda i: (0, 0)),
            pl.BlockSpec((chunk, COLS, cols), lambda i: (i, 0, 0)),
        ],
        out_specs=[
            pl.BlockSpec((COLS, 128), lambda i: (0, 0)),
            pl.BlockSpec((chunk, COLS, cols), lambda i: (i, 0, 0)),
            pl.BlockSpec((chunk, COLS, cols), lambda i: (i, 0, 0)),
            pl.BlockSpec(gram.shape, lambda i: (0, 0)),
        ],
        out_shape=[
            jax.ShapeDtypeStruct((COLS, 128), F32),
            jax.ShapeDtypeStruct((rows, COLS, cols), BF16),
            jax.ShapeDtypeStruct((rows, COLS, cols), BF16),
            jax.ShapeDtypeStruct(gram.shape, F32),
        ],
        scratch_shapes=[
            pltpu.VMEM((2, COLS, 256), BF16),
            pltpu.VMEM((2 * COLS, 2 * COLS), F32),
        ]
        + total.scratch(),
        compiler_params=pltpu.CompilerParams(
            collective_id=1, has_side_effects=True, vmem_limit_bytes=VMEM_LIMIT
        ),
        name="first",
    )(gram, basis)


def second_kernel(chunk, norm, gram, upper_one, high, low, q_ref, r_ref, left):
    step = pl.program_id(0)

    @pl.when(step == 0)
    def _():
        upper, inverse = eliminate(gram[0:COLS, :])
        full = jnp.dot(
            upper[:, 0:COLS], upper_one[...], precision=lax.Precision.HIGHEST,
            preferred_element_type=F32,
        )
        r_ref[...] = full[:, 0:COLS] / norm
        a, b = split(inverse * norm, 2)
        left[...] = spread([a, b, a])

    pad = jnp.zeros((256 - 3 * COLS, high.shape[2]), BF16)
    out = []
    for j in range(chunk):
        hi, lo = high[j], low[j]
        out.append(dot(left[...], jnp.concatenate([hi, hi, lo, pad], axis=0)))
    q_ref[...] = jnp.swapaxes(jnp.stack(out, 0), 0, 1)


def second(gram, upper_one, high, low, norm):
    rows, _, cols = high.shape
    chunk = 8
    return pl.pallas_call(
        functools.partial(second_kernel, chunk, norm),
        grid=(rows // chunk,),
        in_specs=[
            pl.BlockSpec(gram.shape, lambda i: (0, 0)),
            pl.BlockSpec(upper_one.shape, lambda i: (0, 0)),
            pl.BlockSpec((chunk, COLS, cols), lambda i: (i, 0, 0)),
            pl.BlockSpec((chunk, COLS, cols), lambda i: (i, 0, 0)),
        ],
        out_specs=[
            pl.BlockSpec((COLS, chunk, cols), lambda i: (0, i, 0)),
            pl.BlockSpec((COLS, COLS), lambda i: (0, 0)),
        ],
        out_shape=[
            jax.ShapeDtypeStruct((COLS, rows, cols), F32),
            jax.ShapeDtypeStruct((COLS, COLS), F32),
        ],
        scratch_shapes=[pltpu.VMEM((COLS, 256), BF16)],
        compiler_params=pltpu.CompilerParams(vmem_limit_bytes=VMEM_LIMIT),
        name="second",
    )(gram, upper_one, high, low)


def on_device(nx, ny, right_side, center, couplings):
    rows, cols = center.shape
    norm = math.sqrt(rows * cols * nx * ny)
    padded = halo_fields(nx, ny, right_side, center, couplings)
    total = Total(nx, ny)
    basis, gram = powers(total, padded, rows, cols)
    upper_one, high, low, gram = first(total, gram, basis)
    return second(gram, upper_one, high, low, norm)


def solution(mesh):
    placed = (P(None, "gx", "gy"), P("gx", "gy"), P(None, "gx", "gy"))
    return jax.shard_map(
        functools.partial(on_device, mesh.shape["gx"], mesh.shape["gy"]),
        mesh=mesh, in_specs=placed, out_specs=(P(None, "gx", "gy"), P()), check_vma=False,
    )
```

```python
import functools
import math

import jax
import jax.numpy as jnp
from jax import lax
from jax.experimental import pallas as pl
from jax.experimental.pallas import tpu as pltpu
from jax.sharding import PartitionSpec as P

S = 4
B = 16
COLS = B * (S + 1)
F32 = jnp.float32
BF16 = jnp.bfloat16
MESH = pl.DeviceIdType.MESH
VMEM_LIMIT = 56 * 1024 * 1024


def split(x, count):
    parts = []
    for _ in range(count - 1):
        part = x.astype(BF16)
        parts.append(part)
        x = x - part.astype(F32)
    parts.append(x.astype(BF16))
    return parts


def dot(a, b):
    return jnp.dot(a, b, preferred_element_type=F32)


def dot_nt(a, b):
    return lax.dot_general(a, b, (((1,), (1,)), ((), ())), preferred_element_type=F32)


FIELDS = B + 8
SIDES = [(-1, 0), (1, 0), (0, -1), (0, 1), (-1, -1), (-1, 1), (1, -1), (1, 1)]


def halo_kernel(nx, ny, right, center, couplings, out, packs, sides, corners, send, recv):
    gx, gy = lax.axis_index("gx"), lax.axis_index("gy")
    rows, cols = center.shape
    last = cols - 128

    def there(dx, dy):
        ok = None
        for test in ([gx > 0] if dx < 0 else [gx < nx - 1] if dx > 0 else []) + (
            [gy > 0] if dy < 0 else [gy < ny - 1] if dy > 0 else []
        ):
            ok = test if ok is None else jnp.logical_and(ok, test)
        return ok

    def device(dx, dy):
        return (lax.rem(gx + dx + nx, nx), lax.rem(gy + dy + ny, ny))

    barrier = pltpu.get_barrier_semaphore()
    for side in SIDES:
        @pl.when(there(*side))
        def _():
            pl.semaphore_signal(barrier, inc=1, device_id=device(*side), device_id_type=MESH)

    lane = lax.broadcasted_iota(jnp.int32, (FIELDS, 128), 1)
    per = 128 // S
    groups = rows // per
    for g in range(rows // 8):
        cut = pl.ds(8 * g, 8)
        fields = jnp.concatenate(
            [
                right[:, cut, :],
                (center[cut, :] - 5.0)[None],
                couplings[:, cut, :],
                jnp.zeros((FIELDS - B - 5, 8, cols), F32),
            ],
            axis=0,
        )
        out[S + 8 * g : S + 8 * g + 8, :, 0:cols] = jnp.swapaxes(fields, 0, 1)
    for g in range(groups):
        left = jnp.zeros((FIELDS, 128), F32)
        far = jnp.zeros((FIELDS, 128), F32)
        for j in range(per):
            r = S + g * per + j
            here = (lane >= S * j) & (lane < S * j + S)
            a = out[r, :, 0:128]
            z = out[r, :, last : last + 128]
            left = jnp.where(here, pltpu.roll(a, S * j, 1) if j else a, left)
            shift = (S * j + S) % 128
            far = jnp.where(here, pltpu.roll(z, shift, 1) if shift else z, far)
        packs[0, g] = left
        packs[1, g] = far

    near_x = (gx > 0).astype(jnp.int32) + (gx < nx - 1).astype(jnp.int32)
    near_y = (gy > 0).astype(jnp.int32) + (gy < ny - 1).astype(jnp.int32)
    pl.semaphore_wait(barrier, (1 + near_x) * (1 + near_y) - 1)

    ends = groups - 1
    core = pl.ds(0, cols)
    ways = [
        (out.at[pl.ds(S, S), :, core], out.at[pl.ds(rows + S, S), :, core]),
        (out.at[pl.ds(rows, S), :, core], out.at[pl.ds(0, S), :, core]),
        (packs.at[0], sides.at[1]),
        (packs.at[1], sides.at[0]),
        (packs.at[0, 0], corners.at[3]),
        (packs.at[1, 0], corners.at[2]),
        (packs.at[0, ends], corners.at[1]),
        (packs.at[1, ends], corners.at[0]),
    ]
    copies = [
        pltpu.make_async_remote_copy(
            src_ref=src, dst_ref=dst, send_sem=send.at[i], recv_sem=recv.at[i],
            device_id=device(*SIDES[i]), device_id_type=MESH,
        )
        for i, (src, dst) in enumerate(ways)
    ]
    for i, side in enumerate(SIDES):
        @pl.when(there(*side))
        def _():
            copies[i].start()

    for i, (dx, dy) in enumerate(SIDES):
        dst = ways[i][1]
        came = there(-dx, -dy)

        @pl.when(jnp.logical_not(came))
        def _():
            dst[...] = jnp.zeros(dst.shape, F32)

        @pl.when(came)
        def _():
            copies[i].wait_recv()

    def halo(near, far, j):
        a = pltpu.roll(far, (128 - S * j) % 128, 1) if j else far
        shift = (128 - S - S * j) % 128
        z = pltpu.roll(near, shift, 1) if shift else near
        return jnp.where(lane < S, a, jnp.where(lane >= 128 - S, z, 0.0))

    tail = slice(cols, cols + 128)
    for g in range(groups):
        near, far = sides[0, g], sides[1, g]
        for j in range(per):
            out[S + g * per + j, :, tail] = halo(near, far, j)
    for i in range(S):
        out[i, :, tail] = halo(corners[0], corners[1], per - S + i)
        out[rows + S + i, :, tail] = halo(corners[2], corners[3], i)

    for i, side in enumerate(SIDES):
        @pl.when(there(*side))
        def _():
            copies[i].wait_send()


def halo_fields(nx, ny, right_side, center, couplings):
    rows, cols = center.shape
    groups = rows * S // 128
    return pl.pallas_call(
        functools.partial(halo_kernel, nx, ny),
        in_specs=[pl.BlockSpec(memory_space=pltpu.VMEM)] * 3,
        out_specs=pl.BlockSpec(memory_space=pltpu.VMEM),
        out_shape=jax.ShapeDtypeStruct((rows + 2 * S, FIELDS, cols + 128), F32),
        scratch_shapes=[
            pltpu.VMEM((2, groups, FIELDS, 128), F32),
            pltpu.VMEM((2, groups, FIELDS, 128), F32),
            pltpu.VMEM((4, FIELDS, 128), F32),
            pltpu.SemaphoreType.DMA((8,)),
            pltpu.SemaphoreType.DMA((8,)),
        ],
        compiler_params=pltpu.CompilerParams(
            collective_id=2, has_side_effects=True, vmem_limit_bytes=VMEM_LIMIT
        ),
        name="halo",
    )(right_side, center, couplings)


class Total:
    def __init__(self, nx, ny):
        self.nx, self.ny = nx, ny
        self.pad_rows = -(-COLS // (8 * ny)) * 8 * ny
        self.piece = self.pad_rows // ny

    def scratch(self):
        nx, ny = self.nx, self.ny
        return [
            pltpu.VMEM((self.pad_rows, 128), F32),
            pltpu.VMEM((self.pad_rows, 128), F32),
            pltpu.VMEM((ny, self.piece, 128), F32),
            pltpu.VMEM((nx, self.piece, 128), F32),
            pltpu.SemaphoreType.DMA((max(nx, ny),)),
            pltpu.SemaphoreType.DMA((ny,)),
            pltpu.SemaphoreType.DMA((nx,)),
            pltpu.SemaphoreType.DMA((ny,)),
        ]

    def peers(self):
        nx, ny = self.nx, self.ny
        gx, gy = lax.axis_index("gx"), lax.axis_index("gy")
        rows = [(gx, lax.rem(gy + d, ny)) for d in range(1, ny)]
        columns = [(lax.rem(gx + d, nx), gy) for d in range(1, nx)]
        return gx, gy, rows, columns

    def greet(self):
        _, _, rows, columns = self.peers()
        barrier = pltpu.get_barrier_semaphore()
        for peer in rows + columns:
            pl.semaphore_signal(barrier, inc=1, device_id=peer, device_id_type=MESH)

    def run(self, scratch):
        x_ref, out_ref, got_row, got_col, send, r1, r2, r3 = scratch
        gx, gy, rows, columns = self.peers()
        pl.semaphore_wait(pltpu.get_barrier_semaphore(), len(rows) + len(columns))

        def push(src, dst, index, sem, peer):
            copy = pltpu.make_async_remote_copy(
                src_ref=src, dst_ref=dst, send_sem=send.at[index], recv_sem=sem,
                device_id=peer, device_id_type=MESH,
            )
            copy.start()
            return copy

        def part(i):
            return pl.ds(pl.multiple_of(i * self.piece, 8), self.piece)

        copies = [
            push(x_ref.at[part(peer[1])], got_row.at[gy], i, r1.at[i], peer)
            for i, peer in enumerate(rows)
        ]
        got_row[gy] = x_ref[part(gy)]
        for copy in copies:
            copy.wait()
        held = got_row[0]
        for i in range(1, self.ny):
            held = held + got_row[i]
        got_col[gx] = held
        copies = [
            push(got_col.at[gx], got_col.at[gx], i, r2.at[i], peer)
            for i, peer in enumerate(columns)
        ]
        for copy in copies:
            copy.wait()
        held = got_col[0]
        for i in range(1, self.nx):
            held = held + got_col[i]
        out_ref[part(gy)] = held
        copies = [
            push(out_ref.at[part(gy)], out_ref.at[part(gy)], i, r3.at[i], peer)
            for i, peer in enumerate(rows)
        ]
        for copy in copies:
            copy.wait()


def powers_kernel(total, rows, cols, chunk, padded, basis, gram, held, acc, levels, *scratch):
    step = pl.program_id(0)

    @pl.when(step == 0)
    def _():
        total.greet()

    def apply(power, r):
        if power == 1:
            def src(i):
                return padded[i, 0:B, :]
        else:
            def src(i):
                return levels[(power - 1) % 2, i]
        here = src(r)
        width = here.shape[1]

        def coef(j):
            return padded[r, B + j : B + j + 1, :]

        near = coef(1) * src(r - 1) + coef(2) * src(r + 1)
        near = near + coef(3) * pltpu.roll(here, 1, 1)
        near = near + coef(4) * pltpu.roll(here, width - 1, 1)
        return coef(0) * here - near

    @pl.when(step == 0)
    def _():
        acc[...] = jnp.zeros_like(acc)

        def copy_row(r, carry):
            held[r, 0:B, :] = padded[r + S, 0:B, 0:cols]
            return carry

        lax.fori_loop(0, rows, copy_row, 0, unroll=8)
        for power in range(1, S + 1):
            for r in list(range(power, S)) + list(range(rows + S, rows + 2 * S - power)):
                levels[power % 2, r] = apply(power, r)

            def row(r, carry):
                out = apply(power, r + S)
                if power < S:
                    levels[power % 2, r + S] = out
                held[r, B * power : B * power + B, :] = out[:, 0:cols]
                return carry

            lax.fori_loop(0, rows, row, 0, unroll=8)

    basis[...] = held[pl.ds(step * chunk, chunk)]
    part = None
    for j in range(0, chunk, 4):
        wide = jnp.concatenate([held[step * chunk + j + i] for i in range(4)], axis=1)
        stack = jnp.concatenate(split(wide, 3), axis=0)
        add = dot_nt(stack, stack)
        part = add if part is None else part + add
    acc[...] += part

    @pl.when(step == pl.num_programs(0) - 1)
    def _():
        a = acc[...]
        c = COLS

        def block(i, j):
            return a[i * c : i * c + c, j * c : j * c + c]

        small = block(0, 2) + block(2, 0) + block(1, 1)
        own = scratch[0]
        own[...] = jnp.zeros_like(own)
        own[0:c, 0:c] = block(0, 0) + ((block(0, 1) + block(1, 0)) + small)
        total.run(scratch)
        gram[...] = scratch[1][...]


def powers(total, padded, rows, cols):
    pad_rows = total.pad_rows
    chunk = 32
    return pl.pallas_call(
        functools.partial(powers_kernel, total, rows, cols, chunk),
        grid=(rows // chunk,),
        in_specs=[pl.BlockSpec(padded.shape, lambda i: (0, 0, 0))],
        out_specs=[
            pl.BlockSpec((chunk, COLS, cols), lambda i: (i, 0, 0)),
            pl.BlockSpec((pad_rows, 128), lambda i: (0, 0)),
        ],
        out_shape=[
            jax.ShapeDtypeStruct((rows, COLS, cols), F32),
            jax.ShapeDtypeStruct((pad_rows, 128), F32),
        ],
        scratch_shapes=[
            pltpu.VMEM((rows, COLS, cols), F32),
            pltpu.VMEM((3 * COLS, 3 * COLS), F32),
            pltpu.VMEM((2, padded.shape[0], B, padded.shape[2]), F32),
        ]
        + total.scratch(),
        compiler_params=pltpu.CompilerParams(
            collective_id=0, has_side_effects=True, vmem_limit_bytes=VMEM_LIMIT
        ),
        name="powers",
    )(padded)


def eliminate(gram):
    c = COLS
    row_id = lax.broadcasted_iota(jnp.int32, (c, 128), 0)
    lane_id = lax.broadcasted_iota(jnp.int32, (c, 128), 1)
    eye = (row_id == lane_id).astype(F32)
    upper = [gram[8 * t : 8 * t + 8] for t in range(c // 8)]
    lower = [eye[8 * t : 8 * t + 8] for t in range(c // 8)]
    sub = lax.broadcasted_iota(jnp.int32, (8, 128), 0)
    scales = []
    for b in range(c // 8):
        later = range(b, c // 8)
        columns = {
            t: [
                jnp.broadcast_to(upper[t][:, 8 * b + j : 8 * b + j + 1], (8, 128))
                for j in range(8)
            ]
            for t in later
        }
        scale = jnp.zeros((8, 128), F32)
        for j in range(8):
            heads = [columns[b][i][j : j + 1] for i in range(8)]
            inv = 1.0 / heads[j]
            inv = inv * (2.0 - heads[j] * inv)
            scale = jnp.where(sub == j, heads[j], scale)
            row_u, row_l = upper[b][j : j + 1], lower[b][j : j + 1]
            for t in later:
                mult = columns[t][j] * inv
                if t == b:
                    mult = jnp.where(sub > j, mult, 0.0)
                for i in range(j + 1, 8):
                    columns[t][i] = columns[t][i] - mult * heads[i]
                upper[t] = upper[t] - mult * row_u
                lower[t] = lower[t] - mult * row_l
        scales.append(scale)
    pivots = jnp.concatenate(scales, axis=0)
    scale = 1.0 / jnp.sqrt(pivots)
    scale = scale * (1.5 - 0.5 * (pivots * scale) * scale)
    up = jnp.concatenate(upper, axis=0) * scale
    return jnp.where(lane_id >= row_id, up, 0.0), jnp.concatenate(lower, axis=0) * scale


def spread(parts):
    wide = None
    for i, part in enumerate(parts):
        one = jnp.concatenate([part.astype(F32), jnp.zeros_like(part, F32)], axis=1)
        if i:
            one = pltpu.roll(one, COLS * i, 1)
        wide = one if wide is None else wide + one
    return wide.astype(BF16)


def first_kernel(total, chunk, gram, basis, upper_ref, high, low, gram_out, left, acc, *scratch):
    step = pl.program_id(0)

    @pl.when(step == 0)
    def _():
        total.greet()
        acc[...] = jnp.zeros_like(acc)
        upper, inverse = eliminate(gram[0:COLS, :])
        upper_ref[...] = upper
        a, b, c = split(inverse, 3)
        left[0] = spread([a, b, a])
        left[1] = spread([c, b, a])

    pad = jnp.zeros((256 - 3 * COLS, basis.shape[2]), BF16)
    part = None
    for j in range(chunk):
        a, b, c = split(basis[j], 3)
        q = dot(left[0], jnp.concatenate([a, a, b, pad], axis=0))
        q = q + dot(left[1], jnp.concatenate([a, b, c, pad], axis=0))
        hi, lo = split(q, 2)
        high[j] = hi
        low[j] = lo
        stack = jnp.concatenate([hi, lo], axis=0)
        add = dot_nt(stack, stack)
        part = add if part is None else part + add
    acc[...] += part

    @pl.when(step == pl.num_programs(0) - 1)
    def _():
        c = COLS
        a = acc[...]
        own = scratch[0]
        own[...] = jnp.zeros_like(own)
        own[0:c, 0:c] = a[0:c, 0:c] + (
            (a[0:c, c : 2 * c] + a[c : 2 * c, 0:c]) + a[c : 2 * c, c : 2 * c]
        )
        total.run(scratch)
        gram_out[...] = scratch[1][...]


def first(total, gram, basis):
    rows, _, cols = basis.shape
    chunk = 32
    return pl.pallas_call(
        functools.partial(first_kernel, total, chunk),
        grid=(rows // chunk,),
        in_specs=[
            pl.BlockSpec(gram.shape, lambda i: (0, 0)),
            pl.BlockSpec((chunk, COLS, cols), lambda i: (i, 0, 0)),
        ],
        out_specs=[
            pl.BlockSpec((COLS, 128), lambda i: (0, 0)),
            pl.BlockSpec((chunk, COLS, cols), lambda i: (i, 0, 0)),
            pl.BlockSpec((chunk, COLS, cols), lambda i: (i, 0, 0)),
            pl.BlockSpec(gram.shape, lambda i: (0, 0)),
        ],
        out_shape=[
            jax.ShapeDtypeStruct((COLS, 128), F32),
            jax.ShapeDtypeStruct((rows, COLS, cols), BF16),
            jax.ShapeDtypeStruct((rows, COLS, cols), BF16),
            jax.ShapeDtypeStruct(gram.shape, F32),
        ],
        scratch_shapes=[
            pltpu.VMEM((2, COLS, 256), BF16),
            pltpu.VMEM((2 * COLS, 2 * COLS), F32),
        ]
        + total.scratch(),
        compiler_params=pltpu.CompilerParams(
            collective_id=1, has_side_effects=True, vmem_limit_bytes=VMEM_LIMIT
        ),
        name="first",
    )(gram, basis)


def second_kernel(chunk, norm, gram, upper_one, high, low, q_ref, r_ref, left):
    step = pl.program_id(0)

    @pl.when(step == 0)
    def _():
        upper, inverse = eliminate(gram[0:COLS, :])
        full = jnp.dot(
            upper[:, 0:COLS], upper_one[...], precision=lax.Precision.HIGHEST,
            preferred_element_type=F32,
        )
        r_ref[...] = full[:, 0:COLS] / norm
        a, b = split(inverse * norm, 2)
        left[...] = spread([a, b, a])

    pad = jnp.zeros((256 - 3 * COLS, high.shape[2]), BF16)
    out = []
    for j in range(chunk):
        hi, lo = high[j], low[j]
        out.append(dot(left[...], jnp.concatenate([hi, hi, lo, pad], axis=0)))
    q_ref[...] = jnp.swapaxes(jnp.stack(out, 0), 0, 1)


def second(gram, upper_one, high, low, norm):
    rows, _, cols = high.shape
    chunk = 32
    return pl.pallas_call(
        functools.partial(second_kernel, chunk, norm),
        grid=(rows // chunk,),
        in_specs=[
            pl.BlockSpec(gram.shape, lambda i: (0, 0)),
            pl.BlockSpec(upper_one.shape, lambda i: (0, 0)),
            pl.BlockSpec((chunk, COLS, cols), lambda i: (i, 0, 0)),
            pl.BlockSpec((chunk, COLS, cols), lambda i: (i, 0, 0)),
        ],
        out_specs=[
            pl.BlockSpec((COLS, chunk, cols), lambda i: (0, i, 0)),
            pl.BlockSpec((COLS, COLS), lambda i: (0, 0)),
        ],
        out_shape=[
            jax.ShapeDtypeStruct((COLS, rows, cols), F32),
            jax.ShapeDtypeStruct((COLS, COLS), F32),
        ],
        scratch_shapes=[pltpu.VMEM((COLS, 256), BF16)],
        compiler_params=pltpu.CompilerParams(vmem_limit_bytes=VMEM_LIMIT),
        name="second",
    )(gram, upper_one, high, low)


def on_device(nx, ny, right_side, center, couplings):
    rows, cols = center.shape
    norm = math.sqrt(rows * cols * nx * ny)
    padded = halo_fields(nx, ny, right_side, center, couplings)
    total = Total(nx, ny)
    basis, gram = powers(total, padded, rows, cols)
    upper_one, high, low, gram = first(total, gram, basis)
    return second(gram, upper_one, high, low, norm)


def solution(mesh):
    placed = (P(None, "gx", "gy"), P("gx", "gy"), P(None, "gx", "gy"))
    return jax.shard_map(
        functools.partial(on_device, mesh.shape["gx"], mesh.shape["gy"]),
        mesh=mesh, in_specs=placed, out_specs=(P(None, "gx", "gy"), P()), check_vma=False,
    )
```
